32 devices in a mesh: scene: 2 (over x), img: 16 (over z, y, core).
Axes of the slice: x: 2, y: 2, z: 4, core: 2. Of those that a mesh axis runs over, the one named last changes fastest.
Arguments:
- enc_tokens: bfloat16 [1024, 16, 1024], P(('scene', 'img')), parts along dimension 0, may hold values from -6 to 6
- pair_list: int32 [2048, 2], P(('scene', 'img')), parts along dimension 0, may hold values from -1 to 511, as said below
- w_embed: bfloat16 [1024, 768], replicated, may hold values from -0.1875 to 0.1875
- w_query: bfloat16 [768, 768], replicated, may hold values from -0.21875 to 0.21875
- w_key: bfloat16 [768, 768], replicated, may hold values from -0.21875 to 0.21875
- w_value: bfloat16 [768, 768], replicated, may hold values from -0.21875 to 0.21875
- w_out: bfloat16 [768, 768], replicated, may hold values from -0.21875 to 0.21875
- w_head: bfloat16 [768, 28], replicated, may hold values from -0.21875 to 0.21875
Outputs:
- points: float32 [1024, 3, 16], P(('scene', 'img')), parts along dimension 0
- descriptors: float32 [1024, 24, 16], P(('scene', 'img')), parts along dimension 0
- confidence: float32 [1024, 16], P(('scene', 'img')), parts along dimension 0
The draws below stay inside these ranges and needn't reach their ends.
There are 2 independent parts, one for each index of `scene`. The reference program is written for one: setup_inputs(seed, part) draws one part's arguments, and reference() takes and returns one part's arrays. A program takes and returns all parts, laid end to end along the dimension named above; an argument that names none is the same for every part. Nothing has to cross between parts.
Inputs may be any that keep to these rules, and one draw needn't show every extreme that they name: `pair_list`: the 64 rows of one executor (index of img) name in column 0 an image held by that executor and in column 1 a partner image held by another executor; the used rows come first and the rest hold -1 in both columns. Every executor uses 64 - 64 // 4 rows or more, and some executor uses all. The partners that one executor names on one image owner are distinct and at most 5; some executor names 5 on one owner, and some image owner is named 5 times by every other executor.
All inputs are finite; a program needn't handle non-finite values.
Results may differ from the reference program's by a relative error of at most 0.0055.
Values may be sent and summed in bfloat16 or wider, within the bound.
No kernel may reach another device: no remote copies, remote signals or barrier semaphores. Data moves between devices by JAX's collectives and lax.ppermute only.
A program may use at most 128 MiB of HBM per device.

```python
import jax
import jax.numpy as jnp
from jax import lax

D_ENC = 1024
D = 768
HEADS = 12
DESC = 24
P_SIZE = 16
IMG_DEV = 32
PAIR_DEV = 64
IMAGES = 512
PAIRS = 1024
N_IMG = 16


def draw_pair_list(key, part):
    key = jax.random.fold_in(key, 11)
    groups = N_IMG
    per_owner = (PAIR_DEV + groups - 2) // (groups - 1)
    slot_total = (groups - 1) * per_owner
    split_keys = jax.random.split(key, 6)
    hub_owner = jax.random.randint(split_keys[0], (), 0, groups)
    busiest = jax.random.randint(split_keys[1], (), 0, groups)
    executors = jnp.arange(groups, dtype=jnp.int32)
    shuffled = jax.vmap(lambda row_key: jax.random.permutation(row_key, slot_total))(jax.random.split(split_keys[2], groups)).astype(jnp.int32)
    owner_all = (executors[:, None] + shuffled // per_owner + 1) % groups
    position_list = jnp.arange(slot_total, dtype=jnp.int32)[None, :]
    ranking = jnp.where(owner_all == hub_owner, position_list - slot_total, position_list)
    picked = jnp.argsort(ranking, axis=1, stable=True)[:, :PAIR_DEV]
    chosen = jnp.take_along_axis(shuffled, picked, axis=1)
    owner_chosen = (executors[:, None] + chosen // per_owner + 1) % groups
    within = chosen % per_owner
    base_image = jax.random.randint(split_keys[3], (groups, groups), 0, IMG_DEV)
    offset_image = jnp.take_along_axis(base_image, owner_chosen, axis=1)
    partner = owner_chosen * IMG_DEV + (offset_image + within) % IMG_DEV
    used_count = PAIR_DEV - PAIR_DEV // 4 * jax.random.randint(split_keys[4], (groups,), 0, 2)
    used_count = jnp.where(executors == busiest, PAIR_DEV, used_count)
    in_use = jnp.arange(PAIR_DEV, dtype=jnp.int32)[None, :] < used_count[:, None]
    local_image = executors[:, None] * IMG_DEV + jax.random.randint(split_keys[5], (groups, PAIR_DEV), 0, IMG_DEV)
    first_col = jnp.where(in_use, local_image, -1)
    second_col = jnp.where(in_use, partner, -1)
    return jnp.stack([first_col, second_col], axis=-1).reshape(groups * PAIR_DEV, 2).astype(jnp.int32)


def shard_levels(rng, extent, cuts, least, largest):
    level = 1.0
    for axis_at, shards_of in cuts:
        draws = jax.random.uniform(jax.random.fold_in(jax.random.fold_in(rng, 6), axis_at), (shards_of,), jnp.float32, least / len(cuts), largest / len(cuts))
        level = level * jnp.repeat(jnp.exp(draws), extent[axis_at] // shards_of).reshape((-1,) + (1,) * (len(extent) - 1 - axis_at))
    return level


def noise(own_key, extent, width, bound, cuts=(), held_as=jnp.bfloat16):
    array = jax.random.normal(own_key, extent, jnp.float32) * width
    if len(cuts) > 0:
        array = shard_levels(own_key, extent, cuts, -0.22, 0.18) * array
    return jnp.clip(array, min=-bound, max=bound).astype(held_as)


def setup_inputs(seed: int = 0, part: int = 0) -> dict:
    splits = jax.random.split(jax.random.key(seed), 9)
    part_splits = jax.random.split(jax.random.fold_in(splits[8], part), 9)
    enc_tokens = noise(part_splits[0], (IMAGES, P_SIZE, D_ENC), 1.0, 6.0, ((0, 16),))
    pair_list = draw_pair_list(jax.random.fold_in(jax.random.fold_in(splits[8], part), 71), part)
    w_embed = noise(splits[2], (D_ENC, D), D_ENC ** -0.5, 0.1875)
    w_query = noise(splits[3], (D, D), D ** -0.5, 0.21875)
    w_key = noise(splits[4], (D, D), D ** -0.5, 0.21875)
    w_value = noise(splits[5], (D, D), D ** -0.5, 0.21875)
    w_out = noise(splits[6], (D, D), D ** -0.5, 0.21875)
    w_head = noise(splits[7], (D, DESC + 4), D ** -0.5, 0.21875)
    return dict(enc_tokens=enc_tokens, pair_list=pair_list, w_embed=w_embed, w_query=w_query, w_key=w_key, w_value=w_value, w_out=w_out, w_head=w_head)


def layer_norm(field):
    average = lax.optimization_barrier(jnp.mean(field, axis=-1, keepdims=True))
    centred = field - average
    variance = lax.optimization_barrier(jnp.mean(centred * centred, axis=-1, keepdims=True))
    return centred * lax.rsqrt(variance + 1e-06)

def reference(enc_tokens, pair_list, w_embed, w_query, w_key, w_value, w_out, w_head):
    head_dim = D // HEADS
    channels = DESC + 4
    embedded = jnp.dot(enc_tokens.reshape(IMAGES * P_SIZE, D_ENC), w_embed, preferred_element_type=jnp.float32).astype(jnp.bfloat16)
    normed = layer_norm(embedded.astype(jnp.float32)).astype(jnp.bfloat16)
    queries = jnp.dot(normed, w_query, preferred_element_type=jnp.float32).astype(jnp.bfloat16).reshape(IMAGES, P_SIZE, D)
    key_rows = jnp.dot(normed, w_key, preferred_element_type=jnp.float32).astype(jnp.bfloat16).reshape(IMAGES, P_SIZE, D)
    value_rows = jnp.dot(normed, w_value, preferred_element_type=jnp.float32).astype(jnp.bfloat16).reshape(IMAGES, P_SIZE, D)
    embedded = embedded.reshape(IMAGES, P_SIZE, D)
    score_scale = 1.0 / head_dim ** 0.5

    def one_block(pair_rows):
        first_image = jnp.clip(pair_rows[:, 0], 0, IMAGES - 1).astype(jnp.int32)
        second_image = jnp.clip(pair_rows[:, 1], 0, IMAGES - 1).astype(jnp.int32)
        in_use = (pair_rows[:, 1] >= 0).astype(jnp.float32)
        count = pair_rows.shape[0]
        query_heads = queries[second_image].reshape(count, P_SIZE, HEADS, head_dim).astype(jnp.float32)
        key_heads = key_rows[first_image].reshape(count, P_SIZE, HEADS, head_dim).astype(jnp.float32)
        value_heads = value_rows[first_image].reshape(count, P_SIZE, HEADS, head_dim).astype(jnp.float32)
        scores = jnp.einsum('bqhd,bkhd->bhqk', query_heads, key_heads) * score_scale
        exponent = jnp.exp(scores)
        weights = (exponent / lax.optimization_barrier(jnp.sum(exponent, axis=-1, keepdims=True))).astype(jnp.bfloat16)
        attended = jnp.einsum('bhqk,bkhd->bqhd', weights.astype(jnp.float32), value_heads).astype(jnp.bfloat16)
        attended = attended.reshape(count * P_SIZE, D)
        updated = embedded[second_image].reshape(count * P_SIZE, D).astype(jnp.float32) + jnp.dot(attended, w_out, preferred_element_type=jnp.float32)
        head_input = layer_norm(updated).astype(jnp.bfloat16)
        head_out = jnp.dot(head_input, w_head, preferred_element_type=jnp.float32).reshape(count, P_SIZE, channels)
        confidence_weight = 1.0 + jnp.exp(head_out[..., 3:4])
        weighted = jnp.concatenate([confidence_weight * head_out[..., 0:3], confidence_weight * head_out[..., 4:], confidence_weight], axis=-1)
        return weighted * in_use[:, None, None]
    weighted_all = lax.map(one_block, pair_list.reshape(N_IMG, PAIR_DEV, 2))
    weighted_all = weighted_all.reshape(PAIRS, P_SIZE, channels)
    target = jnp.where(pair_list[:, 1] >= 0, pair_list[:, 1], IMAGES).astype(jnp.int32)
    totals = jnp.zeros((IMAGES, P_SIZE, channels), jnp.float32).at[target].add(weighted_all, mode='drop')
    confidence = totals[:, :, channels - 1]
    divisor = 1.0 + confidence[:, :, None]
    points = jnp.transpose(totals[:, :, 0:3] / divisor, (0, 2, 1))
    descriptors = jnp.transpose(totals[:, :, 3:channels - 1] / divisor, (0, 2, 1))
    return (points, descriptors, confidence)
```

```python
import functools
import math

import jax
import jax.numpy as jnp
from jax import lax
from jax.experimental import pallas as pl
from jax.experimental.pallas import tpu as pltpu
from jax.sharding import PartitionSpec as P

HEADS = 12
BF16 = jnp.bfloat16
F32 = jnp.float32
VMEM_LIMIT = 40 * 1024 * 1024


def layer_norm(field):
    average = jnp.mean(field, axis=-1, keepdims=True)
    centred = field - average
    variance = jnp.mean(centred * centred, axis=-1, keepdims=True)
    return centred * lax.rsqrt(variance + 1e-06)


def step_to(owner, position, groups):
    if groups & (groups - 1) == 0:
        return owner ^ position
    return lax.rem(owner - position + groups, groups)


def source_of(step, position, groups):
    if groups & (groups - 1) == 0:
        return step ^ position
    return lax.rem(position - step + groups, groups)


def embed_kernel(groups, per_owner, patches, pairs_ref, enc_ref, w_ref, emb_ref, normed_ref, *rest):
    sends, (slots,) = rest[:-1], rest[-1:]
    img_dev = enc_ref.shape[0] // patches
    position = pairs_ref[0, 0] // img_dev

    @pl.loop(0, groups * per_owner)
    def _(slot):
        slots[slot] = 0

    @pl.loop(0, groups)
    def _(owner):
        slots[groups * per_owner + owner] = 0

    @pl.loop(0, pairs_ref.shape[0])
    def _(row):
        partner = pairs_ref[row, 1]

        @pl.when(partner >= 0)
        def _():
            owner = partner // img_dev
            rank = slots[groups * per_owner + owner]
            slots[groups * per_owner + owner] = rank + 1
            step = step_to(owner, position, groups) if len(sends) > 1 else owner
            slots[step * per_owner + rank] = lax.rem(pairs_ref[row, 0], img_dev)

    embedded = jnp.dot(enc_ref[...], w_ref[...], preferred_element_type=F32).astype(BF16)
    emb_ref[...] = embedded
    normed_ref[...] = layer_norm(embedded.astype(F32)).astype(BF16)

    def image(slot):
        at = pl.multiple_of(slots[slot] * patches, patches)
        return normed_ref[pl.ds(at, patches), :]

    if len(sends) == 1:

        @pl.loop(0, groups * per_owner)
        def _(slot):
            sends[0][pl.ds(pl.multiple_of(slot * patches, patches), patches), :] = image(slot)

    else:
        for step, send in enumerate(sends, 1):
            for rank in range(per_owner):
                send[rank * patches : (rank + 1) * patches, :] = image(step * per_owner + rank)


def query_kernel(scale, normed_ref, w_ref, out_ref):
    rows = jnp.dot(normed_ref[...], w_ref[...], preferred_element_type=F32).astype(BF16)
    out_ref[...] = rows * jnp.asarray(scale, BF16)


def decode_kernel(
    steps, per_owner, patches, table_ref, query_ref, emb_ref, wk_ref, wv_ref, wo_ref, wh_ref, totals_ref, *rest,
):
    blocks, (out_ref, q_rows, e_rows) = rest[:-3], rest[-3:]
    span = per_owner * patches
    width = wk_ref.shape[0]
    pair = 2 * (width // HEADS)

    def partner(step, rank):
        return table_ref[step * per_owner + rank]

    for n, step in enumerate(steps):
        for rank in range(per_owner):
            at = pl.multiple_of(jnp.maximum(partner(step, rank), 0) * patches, patches)
            to = n * span + rank * patches
            q_rows[to : to + patches, :] = query_ref[pl.ds(at, patches), :]
            e_rows[to : to + patches, :] = emb_ref[pl.ds(at, patches), :]

    x = jnp.concatenate([b[...] for b in blocks], axis=0) if len(blocks) > 1 else blocks[0][...]
    keys = jnp.dot(x, wk_ref[...], preferred_element_type=F32).astype(BF16)
    values = jnp.dot(x, wv_ref[...], preferred_element_type=F32).astype(BF16)
    first = lax.broadcasted_iota(jnp.int32, (span, pair), 1) < pair // 2
    at_row = lax.rem(lax.broadcasted_iota(jnp.int32, (2 * span, span), 0), span) // patches
    at_col = lax.broadcasted_iota(jnp.int32, (2 * span, span), 1) // patches
    same = at_row == at_col
    zero = jnp.zeros((), BF16)
    attended = []
    for n in range(len(steps)):
        cut = slice(n * span, (n + 1) * span)
        parts = []
        for p in range(HEADS // 2):
            cols = slice(p * pair, (p + 1) * pair)
            q = q_rows[cut, cols]
            both = jnp.concatenate([jnp.where(first, q, zero), jnp.where(first, zero, q)], axis=0)
            scores = lax.dot_general(
                both, keys[cut, cols], (((1,), (1,)), ((), ())), preferred_element_type=F32
            )
            exponent = jnp.exp(jnp.where(same, scores, -jnp.inf))
            weights = (exponent / jnp.sum(exponent, axis=-1, keepdims=True)).astype(BF16)
            mixed = jnp.dot(weights, values[cut, cols], preferred_element_type=F32)
            parts.append(jnp.where(first, mixed[:span], mixed[span:]).astype(BF16))
        attended.append(jnp.concatenate(parts, axis=1))
    attended = jnp.concatenate(attended, axis=0) if len(attended) > 1 else attended[0]
    updated = e_rows[...].astype(F32) + jnp.dot(attended, wo_ref[...], preferred_element_type=F32)
    head_input = layer_norm(updated).astype(BF16)
    head_out = jnp.dot(head_input, wh_ref[...], preferred_element_type=F32)
    weight = 1.0 + jnp.exp(head_out[:, 3:4])
    column = lax.broadcasted_iota(jnp.int32, head_out.shape, 1)
    terms = jnp.where(column == 3, weight, weight * head_out)
    out_ref[...] = totals_ref[...]
    for n, step in enumerate(steps):
        for rank in range(per_owner):
            image = partner(step, rank)
            to = n * span + rank * patches

            @pl.when(image >= 0)
            def _():
                at = pl.ds(pl.multiple_of(image * patches, patches), patches)
                out_ref[at, :] = out_ref[at, :] + terms[to : to + patches, :]


def vmem():
    return pl.BlockSpec(memory_space=pltpu.VMEM)


def smem():
    return pl.BlockSpec(memory_space=pltpu.SMEM)


def cost(flops, moved):
    return pl.CostEstimate(flops=int(flops), bytes_accessed=int(moved), transcendentals=0)


def per_device(enc_tokens, pair_list, w_embed, w_query, w_key, w_value, w_out, w_head):
    groups = lax.axis_size("img")
    position = lax.axis_index("img")
    img_dev, patches, enc_width = enc_tokens.shape
    width = w_query.shape[0]
    channels = w_head.shape[1]
    pair_dev = pair_list.shape[0]
    per_owner = (pair_dev + groups - 2) // (groups - 1)
    span = per_owner * patches
    own_rows = img_dev * patches
    params = pltpu.CompilerParams(vmem_limit_bytes=VMEM_LIMIT)
    by_permute = groups <= 32

    partners = lax.all_gather(pair_list[:, 1], "img", axis=0)
    mine = (partners // img_dev == position) & (partners >= 0)
    before = jnp.cumsum(mine.astype(jnp.int32), axis=1) - 1
    ranks = jnp.arange(per_owner, dtype=jnp.int32)
    hit = mine[:, None, :] & (before[:, None, :] == ranks[None, :, None])
    table = jnp.sum(jnp.where(hit, (partners % img_dev + 1)[:, None, :], 0), axis=2) - 1
    if by_permute:
        table = table[source_of(jnp.arange(groups, dtype=jnp.int32), position, groups)]
    table = table.reshape(groups * per_owner)

    if by_permute:
        send_shapes = [jax.ShapeDtypeStruct((span, width), BF16)] * (groups - 1)
    else:
        send_shapes = [jax.ShapeDtypeStruct((groups * span, width), BF16)]
    embedded, normed, *sends = pl.pallas_call(
        functools.partial(embed_kernel, groups, per_owner, patches),
        out_shape=[jax.ShapeDtypeStruct((own_rows, width), BF16)] * 2 + send_shapes,
        in_specs=[smem(), vmem(), vmem()],
        out_specs=[vmem()] * (2 + len(send_shapes)),
        scratch_shapes=[pltpu.SMEM((groups * per_owner + groups,), jnp.int32)],
        compiler_params=params,
        cost_estimate=cost(2 * own_rows * enc_width * width, 6e6),
        name="embed",
    )(pair_list, enc_tokens.reshape(own_rows, enc_width), w_embed)

    queries = pl.pallas_call(
        functools.partial(query_kernel, 1.0 / math.sqrt(width // HEADS)),
        out_shape=jax.ShapeDtypeStruct((own_rows, width), BF16),
        in_specs=[vmem(), vmem()],
        out_specs=vmem(),
        compiler_params=params,
        cost_estimate=cost(2 * own_rows * width * width, 3e6),
        name="queries",
    )(normed, w_query)

    def decode(totals, table, steps, blocks):
        count = span * len(steps)
        return pl.pallas_call(
            functools.partial(decode_kernel, steps, per_owner, patches),
            out_shape=jax.ShapeDtypeStruct((own_rows, channels), F32),
            in_specs=[smem()] + [vmem()] * (7 + len(blocks)),
            out_specs=vmem(),
            scratch_shapes=[pltpu.VMEM((count, width), BF16)] * 2,
            compiler_params=params,
            cost_estimate=cost(6 * count * width * width, 6e6),
            name="decode",
        )(table, queries, embedded, w_key, w_value, w_out, w_head, totals, *blocks)

    totals = jnp.zeros((own_rows, channels), F32)
    if by_permute:
        pairs_of = lambda s: [(i, i ^ s if groups & (groups - 1) == 0 else (i + s) % groups) for i in range(groups)]
        half = groups // 2
        near = list(range(2, half)) + [1]
        far = list(range(half, groups))
        got = {}

        def chain(order, window):
            for n, s in enumerate(order):
                v = sends[s - 1]
                if n >= window:
                    back = order[n - window]
                    v, got[back] = lax.optimization_barrier((v, got[back]))
                got[s] = lax.ppermute(v, "img", pairs_of(s))

        chain(far, 3)
        chain(near, 2)
        order = []
        for k in range(half):
            order += far[k : k + 1] + near[k : k + 1]
        for k in range(0, len(order), 2):
            steps = tuple(order[k : k + 2])
            totals = decode(totals, table, steps, [got[s] for s in steps])
    else:
        got = lax.all_to_all(sends[0].reshape(groups, span, width), "img", 0, 0, tiled=True)
        some = math.gcd(groups, max(1, 128 // span))

        def body(k, totals):
            part = lax.dynamic_slice_in_dim(table, k * some * per_owner, some * per_owner)
            block = lax.dynamic_slice_in_dim(got, k * some, some).reshape(some * span, width)
            return decode(totals, part, tuple(range(some)), [block])

        totals = lax.fori_loop(0, groups // some, body, totals)
    totals = jnp.transpose(totals.reshape(img_dev, patches, channels), (0, 2, 1))
    confidence = totals[:, 3, :]
    divisor = 1.0 + confidence[:, None, :]
    return (totals[:, 0:3, :] / divisor, totals[:, 4:, :] / divisor, confidence)


def solution(mesh):
    rows = P(("scene", "img"))
    return jax.shard_map(
        per_device,
        mesh=mesh,
        in_specs=(rows, rows, P(), P(), P(), P(), P(), P()),
        out_specs=(rows, rows, rows),
        check_vma=False,
    )
```

```python
import functools
import math

import jax
import jax.numpy as jnp
from jax import lax
from jax.experimental import pallas as pl
from jax.experimental.pallas import tpu as pltpu
from jax.sharding import PartitionSpec as P

HEADS = 12
LOGIT = 3
BF16 = jnp.bfloat16
F32 = jnp.float32
VMEM_LIMIT = 12 * 1024 * 1024
LARGE_LIMIT = 56 * 1024 * 1024
MOST_GROUPS = 32
LANES = 128
TILE = 16


def layer_norm(field):
    average = jnp.mean(field, axis=-1, keepdims=True)
    centred = field - average
    variance = jnp.mean(centred * centred, axis=-1, keepdims=True)
    return centred * lax.rsqrt(variance + 1e-06)


def block_rows(slots, patches, width):
    return slots * patches * (width // LANES) + TILE


def embed_kernel(
    groups, per_owner, patches, steps, send_rows, pairs_hbm, enc_hbm, w_hbm, emb_hbm, normed_hbm, *rest
):
    sends = rest[: len(send_rows)]
    pairs, slots, ids, ranks, enc, w, emb, normed, filled, in_sem, out_sem = rest[len(send_rows) :]
    img_dev = enc.shape[0] // patches
    width = w.shape[1]
    loads = [
        pltpu.make_async_copy(pairs_hbm, pairs, in_sem.at[0]),
        pltpu.make_async_copy(w_hbm, w, in_sem.at[1]),
        pltpu.make_async_copy(enc_hbm, enc, in_sem.at[2]),
    ]
    for load in loads:
        load.start()
    position = lax.axis_index("img")
    for owner in range(groups):
        ranks[owner] = 0
        for rank in range(per_owner):
            slots[owner * per_owner + rank] = 0
            ids[owner * per_owner + rank] = 0
    loads[0].wait()
    unused = groups * per_owner

    @pl.loop(0, pairs.shape[1], unroll=4)
    def _(row):
        partner = pairs[1, row]
        live = partner >= 0
        owner = jnp.where(live, lax.div(partner, img_dev), groups)
        rank = jnp.where(live, ranks[owner], 0)
        ranks[owner] = rank + 1
        step = owner ^ position if len(send_rows) > 1 else owner
        at = jnp.where(live, step * per_owner + rank, unused)
        slots[at] = lax.rem(jnp.maximum(pairs[0, row], 0), img_dev) * patches
        ids[at] = lax.rem(jnp.maximum(partner, 0), img_dev) + 1

    loads[1].wait()
    loads[2].wait()
    embedded = jnp.dot(enc[...], w[...], preferred_element_type=F32).astype(BF16)
    emb[...] = embedded
    stores = [pltpu.make_async_copy(emb, emb_hbm, out_sem.at[0])]
    stores[-1].start()
    normed[...] = layer_norm(embedded.astype(F32)).astype(BF16)
    stores.append(pltpu.make_async_copy(normed, normed_hbm, out_sem.at[1]))
    stores[-1].start()

    span = per_owner * patches
    tall = block_rows(per_owner, patches, width)
    tile_row = lax.broadcasted_iota(jnp.int32, (TILE, LANES), 0)
    place = {}
    base = 0
    for n, rows in enumerate(send_rows):
        place[(base + rows) // tall - 1] = (n, base, rows)
        base += rows
    for block, step in enumerate(steps):
        top = block * tall
        marks = jnp.zeros((TILE, LANES), F32)
        for rank in range(per_owner):
            slot = step * per_owner + rank
            image = normed[pl.ds(pl.multiple_of(slots[slot], patches), patches), :]
            for f in range(width // LANES):
                to = top + f * span + rank * patches
                filled[to : to + patches, :] = image[:, f * LANES : (f + 1) * LANES]
            marks = jnp.where(tile_row == rank, ids[slot].astype(F32), marks)
        filled[top + tall - TILE : top + tall, :] = marks.astype(BF16)
        if block in place:
            n, base, rows = place[block]
            stores.append(pltpu.make_async_copy(filled.at[pl.ds(base, rows)], sends[n], out_sem.at[2 + n]))
            stores[-1].start()
    for store in stores:
        store.wait()


def join_kernel(copies, *refs):
    *refs, sem = refs
    moves = []
    for n, (source, at, target, to, rows) in enumerate(copies):
        part = refs[source].at[pl.ds(at, rows)]
        moves.append(pltpu.make_async_copy(part, refs[2 + target].at[pl.ds(to, rows)], sem.at[n]))
        moves[-1].start()
    for move in moves:
        move.wait()


def query_kernel(scale, normed_ref, w_ref, out_ref):
    rows = jnp.dot(normed_ref[...], w_ref[...], preferred_element_type=F32).astype(BF16)
    out_ref[...] = rows * jnp.asarray(scale, BF16)


def decode_kernel(
    parts, per_owner, patches, first_call, last_call, query_ref, emb_ref, wk_ref, wv_ref, wo_ref, wh_ref, *rest
):
    rest = list(rest)
    totals_in = None if first_call else rest.pop(0)
    operands = [rest.pop(0) for _ in range(1 + max(n for n, _ in parts))]
    if last_call:
        points_ref, descriptors_ref, confidence_ref, q_rows, e_rows, marks, ids, sem, totals_ref = rest
    else:
        totals_ref, q_rows, e_rows, marks, ids, sem = rest
    width = wk_ref.shape[0]
    pair = 2 * (width // HEADS)
    span = per_owner * patches
    tall = block_rows(per_owner, patches, width)

    rows = []
    for k, (n, block) in enumerate(parts):
        top = block * tall
        mark = operands[n][top + tall - TILE : top + tall, :]
        marks[k * TILE : (k + 1) * TILE, :] = mark.astype(F32).astype(jnp.int32)
        pieces = [operands[n][top + f * span : top + (f + 1) * span, :] for f in range(width // LANES)]
        rows.append(jnp.concatenate(pieces, axis=1))
    to_scalars = pltpu.make_async_copy(marks, ids, sem)
    to_scalars.start()
    x = jnp.concatenate(rows, axis=0) if len(rows) > 1 else rows[0]
    keys = jnp.dot(x, wk_ref[...], preferred_element_type=F32).astype(BF16)
    values = jnp.dot(x, wv_ref[...], preferred_element_type=F32).astype(BF16)

    to_scalars.wait()
    slots = [ids[k * TILE + rank, 0] for k in range(len(parts)) for rank in range(per_owner)]
    for n, mark in enumerate(slots):
        at = pl.ds(pl.multiple_of(jnp.maximum(mark - 1, 0) * patches, patches), patches)
        to = slice(n * patches, (n + 1) * patches)
        q_rows[to, :] = query_ref[at, :]
        e_rows[to, :] = emb_ref[at, :]

    zero = jnp.zeros((), BF16)
    attended = []
    some = span * max(1, LANES // span)
    for start in range(0, x.shape[0], some):
        cut = slice(start, min(start + some, x.shape[0]))
        size = cut.stop - cut.start
        first = lax.broadcasted_iota(jnp.int32, (size, pair), 1) < pair // 2
        at_row = lax.rem(lax.broadcasted_iota(jnp.int32, (2 * size, size), 0), size) // patches
        same = at_row == lax.broadcasted_iota(jnp.int32, (2 * size, size), 1) // patches
        found = []
        for p in range(HEADS // 2):
            cols = slice(p * pair, (p + 1) * pair)
            q = q_rows[cut, cols]
            both = jnp.concatenate([jnp.where(first, q, zero), jnp.where(first, zero, q)], axis=0)
            scores = lax.dot_general(
                both, keys[cut, cols], (((1,), (1,)), ((), ())), preferred_element_type=F32
            )
            exponent = jnp.exp(jnp.where(same, scores, -jnp.inf))
            weights = (exponent / jnp.sum(exponent, axis=-1, keepdims=True)).astype(BF16)
            mixed = jnp.dot(weights, values[cut, cols], preferred_element_type=F32)
            found.append(jnp.where(first, mixed[:size], mixed[size:]).astype(BF16))
        attended.append(jnp.concatenate(found, axis=1))
    attended = jnp.concatenate(attended, axis=0) if len(attended) > 1 else attended[0]
    updated = e_rows[...].astype(F32) + jnp.dot(attended, wo_ref[...], preferred_element_type=F32)
    head_input = layer_norm(updated).astype(BF16)
    head_out = lax.dot_general(
        head_input, wh_ref[...], (((1,), (1,)), ((), ())), preferred_element_type=F32
    )
    weight = 1.0 + jnp.exp(head_out[:, LOGIT : LOGIT + 1])
    column = lax.broadcasted_iota(jnp.int32, head_out.shape, 1)
    terms = jnp.where(column == LOGIT, weight, weight * head_out)
    totals_ref[...] = jnp.zeros(totals_ref.shape, F32) if first_call else totals_in[...]
    for n, mark in enumerate(slots):

        @pl.when(mark > 0)
        def _():
            at = pl.ds(pl.multiple_of((mark - 1) * patches, patches), patches)
            totals_ref[at, :] = totals_ref[at, :] + terms[n * patches : (n + 1) * patches, :]

    if last_call:
        img_dev = confidence_ref.shape[1]
        for token in range(patches):
            rows = jnp.transpose(totals_ref[pl.ds(token, img_dev, stride=patches), :])
            confidence = rows[LOGIT : LOGIT + 1]
            ratio = rows / (1.0 + confidence)
            confidence_ref[token : token + 1, :] = confidence
            for channel in range(LOGIT):
                points_ref[channel, token : token + 1, :] = ratio[channel : channel + 1]
            for channel in range(LOGIT + 1, rows.shape[0]):
                descriptors_ref[channel - LOGIT - 1, token : token + 1, :] = ratio[channel : channel + 1]


def vmem():
    return pl.BlockSpec(memory_space=pltpu.VMEM)


def smem():
    return pl.BlockSpec(memory_space=pltpu.SMEM)


def hbm():
    return pl.BlockSpec(memory_space=pltpu.HBM)


LITTLE = pl.CostEstimate(flops=1, bytes_accessed=1, transcendentals=0)


def per_device(enc_tokens, pair_list, w_embed, w_query, w_key, w_value, w_out, w_head):
    groups = lax.axis_size("img")
    img_dev, patches, enc_width = enc_tokens.shape
    width = w_query.shape[0]
    channels = w_head.shape[1]
    pair_dev = pair_list.shape[0]
    per_owner = (pair_dev + groups - 2) // (groups - 1)
    span = per_owner * patches
    own_rows = img_dev * patches
    params = pltpu.CompilerParams(vmem_limit_bytes=VMEM_LIMIT)
    large = pltpu.CompilerParams(vmem_limit_bytes=LARGE_LIMIT)
    by_permute = groups <= MOST_GROUPS and groups >= 8 and groups & (groups - 1) == 0
    tall = block_rows(per_owner, patches, width)

    def rows_of(count):
        return jax.ShapeDtypeStruct((count, width), BF16)

    def blocks_of(count):
        return jax.ShapeDtypeStruct((count * tall, LANES), BF16)

    chips = groups // 2
    far, near = list(range(chips // 2, chips)), list(range(1, chips // 2))
    if by_permute:
        steps = [2 * t for t in far + near] + [2 * t + 1 for t in range(chips)]
        counts = [chips - 1, chips]
    else:
        steps = list(range(groups))
        counts = [groups]
    embedded, normed, *sends = pl.pallas_call(
        functools.partial(embed_kernel, groups, per_owner, patches, steps, [c * tall for c in counts]),
        out_shape=[rows_of(own_rows)] * 2 + [blocks_of(c) for c in counts],
        in_specs=[hbm()] * 3,
        out_specs=[hbm()] * (2 + len(counts)),
        scratch_shapes=[
            pltpu.SMEM((2, pair_dev), jnp.int32),
            pltpu.SMEM((groups * per_owner + 1,), jnp.int32),
            pltpu.SMEM((groups * per_owner + 1,), jnp.int32),
            pltpu.SMEM((groups + 1,), jnp.int32),
            pltpu.VMEM((own_rows, enc_width), BF16),
            pltpu.VMEM((enc_width, width), BF16),
            pltpu.VMEM((own_rows, width), BF16),
            pltpu.VMEM((own_rows, width), BF16),
            pltpu.VMEM((len(steps) * tall, LANES), BF16),
            pltpu.SemaphoreType.DMA((3,)),
            pltpu.SemaphoreType.DMA((2 + len(counts),)),
        ],
        compiler_params=large,
        cost_estimate=LITTLE,
        name="embed",
    )(pair_list.T, enc_tokens.reshape(own_rows, enc_width), w_embed)

    queries = pl.pallas_call(
        functools.partial(query_kernel, 1.0 / math.sqrt(width // HEADS)),
        out_shape=jax.ShapeDtypeStruct((own_rows, width), BF16),
        in_specs=[vmem(), vmem()],
        out_specs=vmem(),
        compiler_params=params,
        cost_estimate=LITTLE,
        name="queries",
    )(normed, w_query)

    def decode(operands, parts, totals, last_call):
        count = span * len(parts)
        first_call = totals is None
        totals_shape = (own_rows, channels)
        scratch = [pltpu.VMEM((count, width), BF16)] * 2
        scratch.append(pltpu.VMEM((len(parts) * TILE, LANES), jnp.int32))
        scratch.append(pltpu.SMEM((len(parts) * TILE, LANES), jnp.int32))
        scratch.append(pltpu.SemaphoreType.DMA)
        if last_call:
            shapes = [(LOGIT, patches, img_dev), (channels - 1 - LOGIT, patches, img_dev), (patches, img_dev)]
            out_shape = [jax.ShapeDtypeStruct(s, F32) for s in shapes]
            out_specs = [vmem()] * 3
            scratch.append(pltpu.VMEM(totals_shape, F32))
        else:
            out_shape, out_specs = jax.ShapeDtypeStruct(totals_shape, F32), vmem()
        inputs = [queries, embedded, w_key, w_value, w_out, w_head.T]
        inputs += ([] if first_call else [totals]) + operands
        return pl.pallas_call(
            functools.partial(decode_kernel, parts, per_owner, patches, first_call, last_call),
            out_shape=out_shape,
            in_specs=[vmem()] * len(inputs),
            out_specs=out_specs,
            scratch_shapes=scratch,
            compiler_params=params,
            cost_estimate=LITTLE,
            name="decode",
        )(*inputs)

    if by_permute:

        def permute(block, step):
            return lax.ppermute(block, "img", [(i, i ^ step) for i in range(groups)])

        mate = permute(sends[1], 1)
        own, queries = lax.optimization_barrier((sends[0], queries))
        copies = []
        for n, t in enumerate(far + near):
            copies.append((0, n * tall, n, 0, tall))
            copies.append((1, t * tall, n, tall, tall))
        joined = pl.pallas_call(
            functools.partial(join_kernel, copies),
            out_shape=[blocks_of(2)] * (chips - 1),
            in_specs=[vmem()] * 2,
            out_specs=[pl.BlockSpec(memory_space=pl.ANY)] * (chips - 1),
            scratch_shapes=[pltpu.SemaphoreType.DMA((len(copies),))],
            compiler_params=params,
            cost_estimate=LITTLE,
            name="join",
        )(own, mate)
        both = dict(zip(far + near, joined))
        got = {t: permute(both[t], 2 * t) for t in far[:-1] + near}
        totals = decode([mate, got[near[0]]], [(0, 0), (1, 0), (1, 1)], None, False)
        for k in range(1, len(near), 2):
            pair = near[k : k + 2]
            parts = [(n, m) for n in range(len(pair)) for m in (0, 1)]
            totals = decode([got[t] for t in pair], parts, totals, False)
        last = far[-1]
        block, got[far[0]], totals = lax.optimization_barrier((both[last], got[far[0]], totals))
        got[last] = permute(block, 2 * last)
        for pair in (far[:2], far[2:-1], [last]):
            parts = [(n, m) for n in range(len(pair)) for m in (0, 1)]
            totals = decode([got[t] for t in pair], parts, totals, pair == [last])
    else:
        got = lax.all_to_all(sends[0].reshape(groups, tall, LANES), "img", 0, 0, tiled=True)
        some = math.gcd(groups, max(1, LANES // span))

        def decode_some(k, totals, last_call):
            block = lax.dynamic_slice_in_dim(got, k * some, some).reshape(some * tall, LANES)
            return decode([block], [(0, n) for n in range(some)], totals, last_call)

        totals = lax.fori_loop(
            0,
            groups // some - 1,
            lambda k, totals: decode_some(k, totals, False),
            jnp.zeros((own_rows, channels), F32),
        )
        totals = decode_some(groups // some - 1, totals, True)
    points, descriptors, confidence = totals
    return (
        jnp.transpose(points, (2, 0, 1)),
        jnp.transpose(descriptors, (2, 0, 1)),
        jnp.transpose(confidence),
    )


def solution(mesh):
    rows = P(("scene", "img"))
    return jax.shard_map(
        per_device,
        mesh=mesh,
        in_specs=(rows, rows, P(), P(), P(), P(), P(), P()),
        out_specs=(rows, rows, rows),
        check_vma=False,
    )
```

```python
import functools
import math

import jax
import jax.numpy as jnp
from jax import lax
from jax.experimental import pallas as pl
from jax.experimental.pallas import tpu as pltpu
from jax.sharding import PartitionSpec as P

HEADS = 12
LOGIT = 3
BF16 = jnp.bfloat16
F32 = jnp.float32
VMEM_LIMIT = 12 * 1024 * 1024
LARGE_LIMIT = 56 * 1024 * 1024
MOST_GROUPS = 32
LANES = 128
TILE = 16
MARK_BASE = 1024


def layer_norm(field):
    average = jnp.mean(field, axis=-1, keepdims=True)
    centred = field - average
    variance = jnp.mean(centred * centred, axis=-1, keepdims=True)
    return centred * lax.rsqrt(variance + 1e-06)


def block_rows(slots, patches, width):
    return slots * patches * (width // LANES) + TILE


def fill(filled, normed, table, steps, per_owner, patches):
    width = normed.shape[1]
    span = per_owner * patches
    tall = block_rows(per_owner, patches, width)
    tile_row = lax.broadcasted_iota(jnp.int32, (TILE, LANES), 0)
    for block, step in enumerate(steps):
        top = block * tall
        marks = jnp.zeros((TILE, LANES), F32)
        for rank in range(per_owner):
            entry = table[step * per_owner + rank]
            at = pl.multiple_of(lax.div(entry, MARK_BASE) * patches, patches)
            image = normed[pl.ds(at, patches), :]
            for f in range(width // LANES):
                to = top + f * span + rank * patches
                filled[to : to + patches, :] = image[:, f * LANES : (f + 1) * LANES]
            marks = jnp.where(tile_row == rank, lax.rem(entry, MARK_BASE).astype(F32), marks)
        filled[top + tall - TILE : top + tall, :] = marks.astype(BF16)


def embed_kernel(
    groups, per_owner, patches, by_distance, sets, pairs_hbm, enc_hbm, w_hbm, emb_hbm, normed_hbm, *rest
):
    sends = rest[: len(sets)]
    pairs, table, ranks, enc, w, emb, normed, filled, in_sem, out_sem = rest[len(sets) :]
    img_dev = enc.shape[0] // patches
    loads = [
        pltpu.make_async_copy(pairs_hbm, pairs, in_sem.at[0]),
        pltpu.make_async_copy(w_hbm, w, in_sem.at[1]),
        pltpu.make_async_copy(enc_hbm, enc, in_sem.at[2]),
    ]
    for load in loads:
        load.start()
    position = lax.axis_index("img")
    unused = groups * per_owner
    for owner in range(groups):
        ranks[owner] = 0
    for slot in range(unused):
        table[slot] = 0
    loads[0].wait()

    @pl.loop(0, pairs.shape[1], unroll=4)
    def _(row):
        partner = pairs[1, row]
        live = partner >= 0
        owner = jnp.where(live, lax.div(partner, img_dev), groups)
        rank = jnp.where(live, ranks[owner], 0)
        ranks[owner] = rank + 1
        step = owner ^ position if by_distance else owner
        at = jnp.where(live, step * per_owner + rank, unused)
        image = lax.rem(jnp.maximum(pairs[0, row], 0), img_dev)
        table[at] = image * MARK_BASE + lax.rem(jnp.maximum(partner, 0), img_dev) + 1

    loads[1].wait()
    loads[2].wait()
    embedded = jnp.dot(enc[...], w[...], preferred_element_type=F32).astype(BF16)
    emb[...] = embedded
    stores = [pltpu.make_async_copy(emb, emb_hbm, out_sem.at[0])]
    stores[-1].start()
    normed[...] = layer_norm(embedded.astype(F32)).astype(BF16)
    stores.append(pltpu.make_async_copy(normed, normed_hbm, out_sem.at[1]))
    stores[-1].start()
    row = 0
    for n, steps in enumerate(sets):
        rows = sends[n].shape[0]
        part = filled.at[pl.ds(row, rows)]
        fill(part, normed, table, steps, per_owner, patches)
        stores.append(pltpu.make_async_copy(part, sends[n], out_sem.at[2 + n]))
        stores[-1].start()
        row += rows
    for store in stores:
        store.wait()


def load_kernel(from_ref, to_ref, sem):
    move = pltpu.make_async_copy(from_ref, to_ref, sem)
    move.start()
    move.wait()


def join_kernel(copies, *refs):
    for source, at, target, to, rows in copies:
        refs[2 + target][to : to + rows, :] = refs[source][at : at + rows, :]


def query_kernel(scale, normed_ref, w_ref, out_ref):
    rows = jnp.dot(normed_ref[...], w_ref[...], preferred_element_type=F32).astype(BF16)
    out_ref[...] = rows * jnp.asarray(scale, BF16)


def decode_kernel(
    parts, per_owner, patches, first_call, last_call, query_ref, emb_ref, wk_ref, wv_ref, wo_ref, wh_ref, *rest
):
    rest = list(rest)
    totals_in = None if first_call else rest.pop(0)
    operands = [rest.pop(0) for _ in range(1 + max(n for n, _ in parts))]
    if last_call:
        points_ref, descriptors_ref, confidence_ref, q_rows, e_rows, marks, ids, sem, totals_ref = rest
    else:
        totals_ref, q_rows, e_rows, marks, ids, sem = rest
    width = wk_ref.shape[0]
    pair = 2 * (width // HEADS)
    span = per_owner * patches
    tall = block_rows(per_owner, patches, width)

    rows = []
    for k, (n, block) in enumerate(parts):
        top = block * tall
        mark = operands[n][top + tall - TILE : top + tall, :]
        marks[k * TILE : (k + 1) * TILE, :] = mark.astype(F32).astype(jnp.int32)
        pieces = [operands[n][top + f * span : top + (f + 1) * span, :] for f in range(width // LANES)]
        rows.append(jnp.concatenate(pieces, axis=1))
    to_scalars = pltpu.make_async_copy(marks, ids, sem)
    to_scalars.start()
    x = jnp.concatenate(rows, axis=0) if len(rows) > 1 else rows[0]
    keys = jnp.dot(x, wk_ref[...], preferred_element_type=F32).astype(BF16)
    values = jnp.dot(x, wv_ref[...], preferred_element_type=F32).astype(BF16)

    to_scalars.wait()
    slots = [ids[k * TILE + rank, 0] for k in range(len(parts)) for rank in range(per_owner)]
    for n, mark in enumerate(slots):
        at = pl.ds(pl.multiple_of(jnp.maximum(mark - 1, 0) * patches, patches), patches)
        to = slice(n * patches, (n + 1) * patches)
        q_rows[to, :] = query_ref[at, :]
        e_rows[to, :] = emb_ref[at, :]

    zero = jnp.zeros((), BF16)
    attended = []
    some = span * max(1, LANES // span)
    for start in range(0, x.shape[0], some):
        cut = slice(start, min(start + some, x.shape[0]))
        size = cut.stop - cut.start
        first = lax.broadcasted_iota(jnp.int32, (size, pair), 1) < pair // 2
        at_row = lax.rem(lax.broadcasted_iota(jnp.int32, (2 * size, size), 0), size) // patches
        same = at_row == lax.broadcasted_iota(jnp.int32, (2 * size, size), 1) // patches
        found = []
        for p in range(HEADS // 2):
            cols = slice(p * pair, (p + 1) * pair)
            q = q_rows[cut, cols]
            both = jnp.concatenate([jnp.where(first, q, zero), jnp.where(first, zero, q)], axis=0)
            scores = lax.dot_general(
                both, keys[cut, cols], (((1,), (1,)), ((), ())), preferred_element_type=F32
            )
            exponent = jnp.exp(jnp.where(same, scores, -jnp.inf))
            weights = (exponent / jnp.sum(exponent, axis=-1, keepdims=True)).astype(BF16)
            mixed = jnp.dot(weights, values[cut, cols], preferred_element_type=F32)
            found.append(jnp.where(first, mixed[:size], mixed[size:]).astype(BF16))
        attended.append(jnp.concatenate(found, axis=1))
    attended = jnp.concatenate(attended, axis=0) if len(attended) > 1 else attended[0]
    updated = e_rows[...].astype(F32) + jnp.dot(attended, wo_ref[...], preferred_element_type=F32)
    head_input = layer_norm(updated).astype(BF16)
    head_out = lax.dot_general(
        head_input, wh_ref[...], (((1,), (1,)), ((), ())), preferred_element_type=F32
    )
    weight = 1.0 + jnp.exp(head_out[:, LOGIT : LOGIT + 1])
    column = lax.broadcasted_iota(jnp.int32, head_out.shape, 1)
    terms = jnp.where(column == LOGIT, weight, weight * head_out)
    totals_ref[...] = jnp.zeros(totals_ref.shape, F32) if first_call else totals_in[...]
    for n, mark in enumerate(slots):
        at = pl.ds(pl.multiple_of(jnp.maximum(mark - 1, 0) * patches, patches), patches)
        term = terms[n * patches : (n + 1) * patches, :]
        totals_ref[at, :] = totals_ref[at, :] + jnp.where(mark > 0, term, 0.0)

    if last_call:
        img_dev = confidence_ref.shape[1]
        for token in range(patches):
            rows = jnp.transpose(totals_ref[pl.ds(token, img_dev, stride=patches), :])
            confidence = rows[LOGIT : LOGIT + 1]
            ratio = rows / (1.0 + confidence)
            confidence_ref[token : token + 1, :] = confidence
            points_ref[pl.ds(token, LOGIT, stride=patches), :] = ratio[:LOGIT]
            count = rows.shape[0] - LOGIT - 1
            descriptors_ref[pl.ds(token, count, stride=patches), :] = ratio[LOGIT + 1 :]


def vmem():
    return pl.BlockSpec(memory_space=pltpu.VMEM)


def smem():
    return pl.BlockSpec(memory_space=pltpu.SMEM)


def hbm():
    return pl.BlockSpec(memory_space=pltpu.HBM)


LITTLE = pl.CostEstimate(flops=1, bytes_accessed=1, transcendentals=0)


def per_device(enc_tokens, pair_list, w_embed, w_query, w_key, w_value, w_out, w_head):
    groups = lax.axis_size("img")
    img_dev, patches, enc_width = enc_tokens.shape
    width = w_query.shape[0]
    channels = w_head.shape[1]
    pair_dev = pair_list.shape[0]
    per_owner = (pair_dev + groups - 2) // (groups - 1)
    span = per_owner * patches
    own_rows = img_dev * patches
    params = pltpu.CompilerParams(vmem_limit_bytes=VMEM_LIMIT)
    large = pltpu.CompilerParams(vmem_limit_bytes=LARGE_LIMIT)
    by_permute = groups <= MOST_GROUPS and groups >= 8 and groups & (groups - 1) == 0
    tall = block_rows(per_owner, patches, width)

    def rows_of(count):
        return jax.ShapeDtypeStruct((count, width), BF16)

    def blocks_of(count):
        return jax.ShapeDtypeStruct((count * tall, LANES), BF16)

    chips = groups // 2
    far, near = list(range(chips // 2, chips)), list(range(1, chips // 2))
    if by_permute:
        sets = [[2 * t + 1 for t in [0] + far], [2 * far[0]], [2 * t for t in far[1:]]]
        sets += [[2 * t + 1 for t in near], [2 * t for t in near]]
    else:
        sets = [list(range(groups))]
    embedded, normed, *sends = pl.pallas_call(
        functools.partial(embed_kernel, groups, per_owner, patches, by_permute, sets),
        out_shape=[rows_of(own_rows)] * 2 + [blocks_of(len(steps)) for steps in sets],
        in_specs=[hbm()] * 3,
        out_specs=[hbm()] * (2 + len(sets)),
        scratch_shapes=[
            pltpu.SMEM((2, pair_dev), jnp.int32),
            pltpu.SMEM((groups * per_owner + 1,), jnp.int32),
            pltpu.SMEM((groups + 1,), jnp.int32),
            pltpu.VMEM((own_rows, enc_width), BF16),
            pltpu.VMEM((enc_width, width), BF16),
            pltpu.VMEM((own_rows, width), BF16),
            pltpu.VMEM((own_rows, width), BF16),
            pltpu.VMEM((sum(len(steps) for steps in sets) * tall, LANES), BF16),
            pltpu.SemaphoreType.DMA((3,)),
            pltpu.SemaphoreType.DMA((2 + len(sets),)),
        ],
        compiler_params=large,
        cost_estimate=LITTLE,
        name="embed",
    )(pair_list.T, enc_tokens.reshape(own_rows, enc_width), w_embed)

    queries = pl.pallas_call(
        functools.partial(query_kernel, 1.0 / math.sqrt(width // HEADS)),
        out_shape=rows_of(own_rows),
        in_specs=[vmem()] * 2,
        out_specs=vmem(),
        compiler_params=params,
        cost_estimate=LITTLE,
        name="queries",
    )(normed, w_query)

    def decode(operands, parts, totals, last_call):
        count = span * len(parts)
        first_call = totals is None
        totals_shape = (own_rows, channels)
        scratch = [pltpu.VMEM((count, width), BF16)] * 2
        scratch.append(pltpu.VMEM((len(parts) * TILE, LANES), jnp.int32))
        scratch.append(pltpu.SMEM((len(parts) * TILE, LANES), jnp.int32))
        scratch.append(pltpu.SemaphoreType.DMA)
        if last_call:
            shapes = [(LOGIT * patches, img_dev), ((channels - 1 - LOGIT) * patches, img_dev), (patches, img_dev)]
            out_shape = [jax.ShapeDtypeStruct(s, F32) for s in shapes]
            out_specs = [vmem()] * 3
            scratch.append(pltpu.VMEM(totals_shape, F32))
        else:
            out_shape, out_specs = jax.ShapeDtypeStruct(totals_shape, F32), vmem()
        inputs = [queries, embedded, w_key, w_value, w_out, w_head.T]
        inputs += ([] if first_call else [totals]) + operands
        return pl.pallas_call(
            functools.partial(decode_kernel, parts, per_owner, patches, first_call, last_call),
            out_shape=out_shape,
            in_specs=[vmem()] * len(inputs),
            out_specs=out_specs,
            scratch_shapes=scratch,
            compiler_params=params,
            cost_estimate=LITTLE,
            name="decode",
        )(*inputs)

    if by_permute:

        def permute(block, step):
            return lax.ppermute(block, "img", [(i, i ^ step) for i in range(groups)])

        mate_far, mate_near = permute(sends[0], 1), permute(sends[3], 1)
        first = permute(sends[1], 2 * far[0])
        own_far = pl.pallas_call(
            load_kernel,
            out_shape=blocks_of(len(far) - 1),
            in_specs=[hbm()],
            out_specs=vmem(),
            scratch_shapes=[pltpu.SemaphoreType.DMA],
            compiler_params=params,
            cost_estimate=LITTLE,
            name="load",
        )(sends[2])

        def join(own, mate, counts, copies):
            copies = [(n, at * tall, target, to * tall, tall) for n, at, target, to in copies]
            return pl.pallas_call(
                functools.partial(join_kernel, copies),
                out_shape=[blocks_of(c) for c in counts],
                in_specs=[vmem()] * 2,
                out_specs=[vmem()] * len(counts),
                compiler_params=params,
                cost_estimate=LITTLE,
                name="join",
            )(own, mate)

        copies = []
        for n in range(len(far) - 1):
            copies += [(0, n, n, 0), (1, n + 2, n, 1)]
        copies.append((1, 1, len(far) - 1, 0))
        *both, late = join(own_far, mate_far, [2] * (len(far) - 1) + [1], copies)
        both = dict(zip(far[1:], both))
        copies = []
        for n in range(len(near)):
            copies += [(0, n, n, 0), (1, n, n, 1)]
        both.update(zip(near, join(sends[4], mate_near, [2] * len(near), copies)))

        got = {far[1]: permute(both[far[1]], 2 * far[1])}
        for t in near:
            got[t] = permute(both[t], 2 * t)
        totals = decode([mate_far], [(0, 0)], None, False)
        block, first, totals = lax.optimization_barrier((both[far[2]], first, totals))
        got[far[2]] = permute(block, 2 * far[2])
        totals = decode([first], [(0, 0)], totals, False)
        for n in range(3, len(far)):
            block, got[far[n - 2]], totals = lax.optimization_barrier((both[far[n]], got[far[n - 2]], totals))
            got[far[n]] = permute(block, 2 * far[n])
        totals = decode([got[far[1]]], [(0, 0), (0, 1)], totals, False)
        late, got[far[-2]], totals = lax.optimization_barrier((late, got[far[-2]], totals))
        last = permute(late, 2 * far[0])
        plan = [near[:2], near[2:]] + [[t] for t in far[2:]]
        for pair in plan:
            parts = [(n, m) for n in range(len(pair)) for m in (0, 1)]
            totals = decode([got[t] for t in pair], parts, totals, False)
        totals = decode([last], [(0, 0)], totals, True)
    else:
        got = lax.all_to_all(sends[0].reshape(groups, tall, LANES), "img", 0, 0, tiled=True)
        some = math.gcd(groups, max(1, LANES // span))

        def decode_some(k, totals, last_call):
            block = lax.dynamic_slice_in_dim(got, k * some, some).reshape(some * tall, LANES)
            return decode([block], [(0, n) for n in range(some)], totals, last_call)

        totals = lax.fori_loop(
            0,
            groups // some - 1,
            lambda k, totals: decode_some(k, totals, False),
            jnp.zeros((own_rows, channels), F32),
        )
        totals = decode_some(groups // some - 1, totals, True)
    points, descriptors, confidence = totals
    return (
        jnp.transpose(points.reshape(LOGIT, patches, img_dev), (2, 0, 1)),
        jnp.transpose(descriptors.reshape(channels - 1 - LOGIT, patches, img_dev), (2, 0, 1)),
        jnp.transpose(confidence),
    )


def solution(mesh):
    rows = P(("scene", "img"))
    return jax.shard_map(
        per_device,
        mesh=mesh,
        in_specs=(rows, rows, P(), P(), P(), P(), P(), P()),
        out_specs=(rows, rows, rows),
        check_vma=False,
    )
```

```python
import functools
import math

import jax
import jax.numpy as jnp
from jax import lax
from jax.experimental import pallas as pl
from jax.experimental.pallas import tpu as pltpu
from jax.sharding import PartitionSpec as P

HEADS = 12
LOGIT = 3
BF16 = jnp.bfloat16
F32 = jnp.float32
VMEM_LIMIT = 12 * 1024 * 1024
LARGE_LIMIT = 56 * 1024 * 1024
MOST_GROUPS = 32
LANES = 128
TILE = 16
MARK_BASE = 1024


def layer_norm(field):
    average = jnp.mean(field, axis=-1, keepdims=True)
    centred = field - average
    variance = jnp.mean(centred * centred, axis=-1, keepdims=True)
    return centred * lax.rsqrt(variance + 1e-06)


def block_rows(slots, patches, width):
    return slots * patches * (width // LANES) + TILE


def fill(filled, normed, table, steps, per_owner, patches):
    width = normed.shape[1]
    span = per_owner * patches
    tall = block_rows(per_owner, patches, width)
    tile_row = lax.broadcasted_iota(jnp.int32, (TILE, LANES), 0)
    for block, step in enumerate(steps):
        top = block * tall
        marks = jnp.zeros((TILE, LANES), F32)
        for rank in range(per_owner):
            entry = table[step * per_owner + rank]
            at = pl.multiple_of(lax.div(entry, MARK_BASE) * patches, patches)
            image = normed[pl.ds(at, patches), :]
            for f in range(width // LANES):
                to = top + f * span + rank * patches
                filled[to : to + patches, :] = image[:, f * LANES : (f + 1) * LANES]
            marks = jnp.where(tile_row == rank, lax.rem(entry, MARK_BASE).astype(F32), marks)
        filled[top + tall - TILE : top + tall, :] = marks.astype(BF16)


def embed_kernel(
    groups, per_owner, patches, by_distance, sets, pairs_hbm, enc_hbm, w_hbm, emb_hbm, normed_hbm, *rest
):
    sends = rest[: len(sets)]
    pairs, table, ranks, enc, w, emb, normed, filled, in_sem, out_sem = rest[len(sets) :]
    img_dev = enc.shape[0] // patches
    loads = [
        pltpu.make_async_copy(pairs_hbm, pairs, in_sem.at[0]),
        pltpu.make_async_copy(w_hbm, w, in_sem.at[1]),
        pltpu.make_async_copy(enc_hbm, enc, in_sem.at[2]),
    ]
    for load in loads:
        load.start()
    position = lax.axis_index("img")
    unused = groups * per_owner
    for owner in range(groups):
        ranks[owner] = 0
    for slot in range(unused):
        table[slot] = 0
    loads[0].wait()

    @pl.loop(0, pairs.shape[1], unroll=4)
    def _(row):
        partner = pairs[1, row]
        live = partner >= 0
        owner = jnp.where(live, lax.div(partner, img_dev), groups)
        rank = jnp.where(live, ranks[owner], 0)
        ranks[owner] = rank + 1
        step = owner ^ position if by_distance else owner
        at = jnp.where(live, step * per_owner + rank, unused)
        image = lax.rem(jnp.maximum(pairs[0, row], 0), img_dev)
        table[at] = image * MARK_BASE + lax.rem(jnp.maximum(partner, 0), img_dev) + 1

    loads[1].wait()
    loads[2].wait()
    embedded = jnp.dot(enc[...], w[...], preferred_element_type=F32).astype(BF16)
    emb[...] = embedded
    stores = [pltpu.make_async_copy(emb, emb_hbm, out_sem.at[0])]
    stores[-1].start()
    normed[...] = layer_norm(embedded.astype(F32)).astype(BF16)
    stores.append(pltpu.make_async_copy(normed, normed_hbm, out_sem.at[1]))
    stores[-1].start()
    row = 0
    for n, steps in enumerate(sets):
        rows = sends[n].shape[0]
        part = filled.at[pl.ds(row, rows)]
        fill(part, normed, table, steps, per_owner, patches)
        stores.append(pltpu.make_async_copy(part, sends[n], out_sem.at[2 + n]))
        stores[-1].start()
        row += rows
    for store in stores:
        store.wait()


def load_kernel(from_ref, to_ref, sem):
    move = pltpu.make_async_copy(from_ref, to_ref, sem)
    move.start()
    move.wait()


def join_kernel(copies, *refs):
    for source, at, target, to, rows in copies:
        refs[2 + target][to : to + rows, :] = refs[source][at : at + rows, :]


def query_kernel(scale, normed_ref, w_ref, out_ref):
    rows = jnp.dot(normed_ref[...], w_ref[...], preferred_element_type=F32).astype(BF16)
    out_ref[...] = rows * jnp.asarray(scale, BF16)


def decode_kernel(
    parts, per_owner, patches, first_call, last_call, query_ref, emb_ref, wk_ref, wv_ref, wo_ref, wh_ref, *rest
):
    rest = list(rest)
    totals_in = None if first_call else rest.pop(0)
    operands = [rest.pop(0) for _ in range(1 + max(n for n, _ in parts))]
    if last_call:
        points_ref, descriptors_ref, confidence_ref, q_rows, e_rows, marks, ids, sem, totals_ref = rest
    else:
        totals_ref, q_rows, e_rows, marks, ids, sem = rest
    width = wk_ref.shape[0]
    pair = 2 * (width // HEADS)
    span = per_owner * patches
    tall = block_rows(per_owner, patches, width)

    rows = []
    for k, (n, block) in enumerate(parts):
        top = block * tall
        mark = operands[n][top + tall - TILE : top + tall, :]
        marks[k * TILE : (k + 1) * TILE, :] = mark.astype(F32).astype(jnp.int32)
        pieces = [operands[n][top + f * span : top + (f + 1) * span, :] for f in range(width // LANES)]
        rows.append(jnp.concatenate(pieces, axis=1))
    to_scalars = pltpu.make_async_copy(marks, ids, sem)
    to_scalars.start()
    x = jnp.concatenate(rows, axis=0) if len(rows) > 1 else rows[0]
    keys = jnp.dot(x, wk_ref[...], preferred_element_type=F32).astype(BF16)
    values = jnp.dot(x, wv_ref[...], preferred_element_type=F32).astype(BF16)

    to_scalars.wait()
    slots = [ids[k * TILE + rank, 0] for k in range(len(parts)) for rank in range(per_owner)]
    for n, mark in enumerate(slots):
        at = pl.ds(pl.multiple_of(jnp.maximum(mark - 1, 0) * patches, patches), patches)
        to = slice(n * patches, (n + 1) * patches)
        q_rows[to, :] = query_ref[at, :]
        e_rows[to, :] = emb_ref[at, :]

    zero = jnp.zeros((), BF16)
    attended = []
    some = span * max(1, LANES // span)
    for start in range(0, x.shape[0], some):
        cut = slice(start, min(start + some, x.shape[0]))
        size = cut.stop - cut.start
        first = lax.broadcasted_iota(jnp.int32, (size, pair), 1) < pair // 2
        at_row = lax.rem(lax.broadcasted_iota(jnp.int32, (2 * size, size), 0), size) // patches
        same = at_row == lax.broadcasted_iota(jnp.int32, (2 * size, size), 1) // patches
        found = []
        for p in range(HEADS // 2):
            cols = slice(p * pair, (p + 1) * pair)
            q = q_rows[cut, cols]
            both = jnp.concatenate([jnp.where(first, q, zero), jnp.where(first, zero, q)], axis=0)
            scores = lax.dot_general(
                both, keys[cut, cols], (((1,), (1,)), ((), ())), preferred_element_type=F32
            )
            exponent = jnp.exp(jnp.where(same, scores, -jnp.inf))
            weights = (exponent / jnp.sum(exponent, axis=-1, keepdims=True)).astype(BF16)
            mixed = jnp.dot(weights, values[cut, cols], preferred_element_type=F32)
            found.append(jnp.where(first, mixed[:size], mixed[size:]).astype(BF16))
        attended.append(jnp.concatenate(found, axis=1))
    attended = jnp.concatenate(attended, axis=0) if len(attended) > 1 else attended[0]
    updated = e_rows[...].astype(F32) + jnp.dot(attended, wo_ref[...], preferred_element_type=F32)
    head_input = layer_norm(updated).astype(BF16)
    head_out = lax.dot_general(
        head_input, wh_ref[...], (((1,), (1,)), ((), ())), preferred_element_type=F32
    )
    weight = 1.0 + jnp.exp(head_out[:, LOGIT : LOGIT + 1])
    column = lax.broadcasted_iota(jnp.int32, head_out.shape, 1)
    terms = jnp.where(column == LOGIT, weight, weight * head_out)
    totals_ref[...] = jnp.zeros(totals_ref.shape, F32) if first_call else totals_in[...]
    for n, mark in enumerate(slots):
        at = pl.ds(pl.multiple_of(jnp.maximum(mark - 1, 0) * patches, patches), patches)
        term = terms[n * patches : (n + 1) * patches, :]
        totals_ref[at, :] = totals_ref[at, :] + jnp.where(mark > 0, term, 0.0)

    if last_call:
        img_dev = confidence_ref.shape[1]
        for token in range(patches):
            rows = jnp.transpose(totals_ref[pl.ds(token, img_dev, stride=patches), :])
            confidence = rows[LOGIT : LOGIT + 1]
            ratio = rows / (1.0 + confidence)
            confidence_ref[token : token + 1, :] = confidence
            points_ref[pl.ds(token, LOGIT, stride=patches), :] = ratio[:LOGIT]
            count = rows.shape[0] - LOGIT - 1
            descriptors_ref[pl.ds(token, count, stride=patches), :] = ratio[LOGIT + 1 :]


def vmem():
    return pl.BlockSpec(memory_space=pltpu.VMEM)


def smem():
    return pl.BlockSpec(memory_space=pltpu.SMEM)


def hbm():
    return pl.BlockSpec(memory_space=pltpu.HBM)


LITTLE = pl.CostEstimate(flops=1, bytes_accessed=1, transcendentals=0)


def per_device(enc_tokens, pair_list, w_embed, w_query, w_key, w_value, w_out, w_head):
    groups = lax.axis_size("img")
    img_dev, patches, enc_width = enc_tokens.shape
    width = w_query.shape[0]
    channels = w_head.shape[1]
    pair_dev = pair_list.shape[0]
    per_owner = (pair_dev + groups - 2) // (groups - 1)
    span = per_owner * patches
    own_rows = img_dev * patches
    params = pltpu.CompilerParams(vmem_limit_bytes=VMEM_LIMIT)
    large = pltpu.CompilerParams(vmem_limit_bytes=LARGE_LIMIT)
    by_permute = groups <= MOST_GROUPS and groups >= 8 and groups & (groups - 1) == 0
    tall = block_rows(per_owner, patches, width)

    def rows_of(count):
        return jax.ShapeDtypeStruct((count, width), BF16)

    def blocks_of(count):
        return jax.ShapeDtypeStruct((count * tall, LANES), BF16)

    chips = groups // 2
    far, near = list(range(chips // 2, chips)), list(range(1, chips // 2))
    if by_permute:
        sets = [[2 * t + 1 for t in [0] + far], [2 * far[0]], [2 * t for t in far[1:]]]
        sets += [[2 * t + 1 for t in near], [2 * t for t in near]]
    else:
        sets = [list(range(groups))]
    embedded, normed, *sends = pl.pallas_call(
        functools.partial(embed_kernel, groups, per_owner, patches, by_permute, sets),
        out_shape=[rows_of(own_rows)] * 2 + [blocks_of(len(steps)) for steps in sets],
        in_specs=[hbm()] * 3,
        out_specs=[hbm()] * (2 + len(sets)),
        scratch_shapes=[
            pltpu.SMEM((2, pair_dev), jnp.int32),
            pltpu.SMEM((groups * per_owner + 1,), jnp.int32),
            pltpu.SMEM((groups + 1,), jnp.int32),
            pltpu.VMEM((own_rows, enc_width), BF16),
            pltpu.VMEM((enc_width, width), BF16),
            pltpu.VMEM((own_rows, width), BF16),
            pltpu.VMEM((own_rows, width), BF16),
            pltpu.VMEM((sum(len(steps) for steps in sets) * tall, LANES), BF16),
            pltpu.SemaphoreType.DMA((3,)),
            pltpu.SemaphoreType.DMA((2 + len(sets),)),
        ],
        compiler_params=large,
        cost_estimate=LITTLE,
        name="embed",
    )(pair_list.T, enc_tokens.reshape(own_rows, enc_width), w_embed)

    queries = pl.pallas_call(
        functools.partial(query_kernel, 1.0 / math.sqrt(width // HEADS)),
        out_shape=rows_of(own_rows),
        in_specs=[vmem()] * 2,
        out_specs=vmem(),
        compiler_params=params,
        cost_estimate=LITTLE,
        name="queries",
    )(normed, w_query)

    def decode(operands, parts, totals, last_call):
        count = span * len(parts)
        first_call = totals is None
        totals_shape = (own_rows, channels)
        scratch = [pltpu.VMEM((count, width), BF16)] * 2
        scratch.append(pltpu.VMEM((len(parts) * TILE, LANES), jnp.int32))
        scratch.append(pltpu.SMEM((len(parts) * TILE, LANES), jnp.int32))
        scratch.append(pltpu.SemaphoreType.DMA)
        if last_call:
            shapes = [(LOGIT * patches, img_dev), ((channels - 1 - LOGIT) * patches, img_dev), (patches, img_dev)]
            out_shape = [jax.ShapeDtypeStruct(s, F32) for s in shapes]
            out_specs = [vmem()] * 3
            scratch.append(pltpu.VMEM(totals_shape, F32))
        else:
            out_shape, out_specs = jax.ShapeDtypeStruct(totals_shape, F32), vmem()
        inputs = [queries, embedded, w_key, w_value, w_out, w_head.T]
        inputs += ([] if first_call else [totals]) + operands
        return pl.pallas_call(
            functools.partial(decode_kernel, parts, per_owner, patches, first_call, last_call),
            out_shape=out_shape,
            in_specs=[vmem()] * len(inputs),
            out_specs=out_specs,
            scratch_shapes=scratch,
            compiler_params=params,
            cost_estimate=LITTLE,
            name="decode",
        )(*inputs)

    if by_permute:

        def permute(block, step):
            return lax.ppermute(block, "img", [(i, i ^ step) for i in range(groups)])

        mate_far, mate_near = permute(sends[0], 1), permute(sends[3], 1)
        first = permute(sends[1], 2 * far[0])
        own_far = pl.pallas_call(
            load_kernel,
            out_shape=blocks_of(len(far) - 1),
            in_specs=[hbm()],
            out_specs=vmem(),
            scratch_shapes=[pltpu.SemaphoreType.DMA],
            compiler_params=params,
            cost_estimate=LITTLE,
            name="load",
        )(sends[2])

        def join(own, mate, counts, copies):
            copies = [(n, at * tall, target, to * tall, tall) for n, at, target, to in copies]
            return pl.pallas_call(
                functools.partial(join_kernel, copies),
                out_shape=[blocks_of(c) for c in counts],
                in_specs=[vmem()] * 2,
                out_specs=[vmem()] * len(counts),
                compiler_params=params,
                cost_estimate=LITTLE,
                name="join",
            )(own, mate)

        copies = []
        for n in range(len(far) - 1):
            copies += [(0, n, n, 0), (1, n + 2, n, 1)]
        copies.append((1, 1, len(far) - 1, 0))
        *both, late = join(own_far, mate_far, [2] * (len(far) - 1) + [1], copies)
        both = dict(zip(far[1:], both))
        copies = []
        for n in range(len(near)):
            copies += [(0, n, n, 0), (1, n, n, 1)]
        both.update(zip(near, join(sends[4], mate_near, [2] * len(near), copies)))

        got = {far[1]: permute(both[far[1]], 2 * far[1])}
        for n, t in enumerate(near):
            block = both[t]
            if n > 1:
                block, got[near[n - 2]] = lax.optimization_barrier((block, got[near[n - 2]]))
            got[t] = permute(block, 2 * t)
        totals = decode([mate_far], [(0, 0)], None, False)
        block, first, totals = lax.optimization_barrier((both[far[2]], first, totals))
        got[far[2]] = permute(block, 2 * far[2])
        totals = decode([first], [(0, 0)], totals, False)
        for n in range(3, len(far)):
            block, got[far[n - 2]], totals = lax.optimization_barrier((both[far[n]], got[far[n - 2]], totals))
            got[far[n]] = permute(block, 2 * far[n])
        totals = decode([got[far[1]]], [(0, 0), (0, 1)], totals, False)
        late, got[far[-2]], totals = lax.optimization_barrier((late, got[far[-2]], totals))
        last = permute(late, 2 * far[0])
        plan = [near[:2], far[2:3], near[2:]] + [[t] for t in far[3:]]
        for pair in plan:
            parts = [(n, m) for n in range(len(pair)) for m in (0, 1)]
            totals = decode([got[t] for t in pair], parts, totals, False)
        totals = decode([last], [(0, 0)], totals, True)
    else:
        got = lax.all_to_all(sends[0].reshape(groups, tall, LANES), "img", 0, 0, tiled=True)
        some = math.gcd(groups, max(1, LANES // span))

        def decode_some(k, totals, last_call):
            block = lax.dynamic_slice_in_dim(got, k * some, some).reshape(some * tall, LANES)
            return decode([block], [(0, n) for n in range(some)], totals, last_call)

        totals = lax.fori_loop(
            0,
            groups // some - 1,
            lambda k, totals: decode_some(k, totals, False),
            jnp.zeros((own_rows, channels), F32),
        )
        totals = decode_some(groups // some - 1, totals, True)
    points, descriptors, confidence = totals
    return (
        jnp.transpose(points.reshape(LOGIT, patches, img_dev), (2, 0, 1)),
        jnp.transpose(descriptors.reshape(channels - 1 - LOGIT, patches, img_dev), (2, 0, 1)),
        jnp.transpose(confidence),
    )


def solution(mesh):
    rows = P(("scene", "img"))
    return jax.shard_map(
        per_device,
        mesh=mesh,
        in_specs=(rows, rows, P(), P(), P(), P(), P(), P()),
        out_specs=(rows, rows, rows),
        check_vma=False,
    )
```

```python
import functools
import math

import jax
import jax.numpy as jnp
from jax import lax
from jax.experimental import pallas as pl
from jax.experimental.pallas import tpu as pltpu
from jax.sharding import PartitionSpec as P

HEADS = 12
LOGIT = 3
BF16 = jnp.bfloat16
F32 = jnp.float32
VMEM_LIMIT = 12 * 1024 * 1024
LARGE_LIMIT = 56 * 1024 * 1024
MOST_GROUPS = 32
LANES = 128
TILE = 16
MARK_BASE = 1024


def layer_norm(field):
    average = jnp.mean(field, axis=-1, keepdims=True)
    centred = field - average
    variance = jnp.mean(centred * centred, axis=-1, keepdims=True)
    return centred * lax.rsqrt(variance + 1e-06)


def block_rows(slots, patches, width):
    return slots * patches * (width // LANES) + TILE


def fill(filled, normed, table, steps, per_owner, patches):
    width = normed.shape[1]
    span = per_owner * patches
    tall = block_rows(per_owner, patches, width)
    tile_row = lax.broadcasted_iota(jnp.int32, (TILE, LANES), 0)
    for block, step in enumerate(steps):
        top = block * tall
        marks = jnp.zeros((TILE, LANES), F32)
        for rank in range(per_owner):
            entry = table[step * per_owner + rank]
            at = pl.multiple_of(lax.div(entry, MARK_BASE) * patches, patches)
            image = normed[pl.ds(at, patches), :]
            for f in range(width // LANES):
                to = top + f * span + rank * patches
                filled[to : to + patches, :] = image[:, f * LANES : (f + 1) * LANES]
            marks = jnp.where(tile_row == rank, lax.rem(entry, MARK_BASE).astype(F32), marks)
        filled[top + tall - TILE : top + tall, :] = marks.astype(BF16)


def embed_kernel(
    groups, per_owner, patches, by_distance, sets, pairs_hbm, enc_hbm, w_hbm, emb_hbm, normed_hbm, *rest
):
    sends = rest[: len(sets)]
    pairs, table, ranks, enc, w, emb, normed, filled, in_sem, out_sem = rest[len(sets) :]
    img_dev = enc.shape[0] // patches
    loads = [
        pltpu.make_async_copy(pairs_hbm, pairs, in_sem.at[0]),
        pltpu.make_async_copy(w_hbm, w, in_sem.at[1]),
        pltpu.make_async_copy(enc_hbm, enc, in_sem.at[2]),
    ]
    for load in loads:
        load.start()
    position = lax.axis_index("img")
    unused = groups * per_owner
    for owner in range(groups):
        ranks[owner] = 0
    for slot in range(unused):
        table[slot] = 0
    loads[0].wait()

    @pl.loop(0, pairs.shape[1], unroll=4)
    def _(row):
        partner = pairs[1, row]
        live = partner >= 0
        owner = jnp.where(live, lax.div(partner, img_dev), groups)
        rank = jnp.where(live, ranks[owner], 0)
        ranks[owner] = rank + 1
        step = owner ^ position if by_distance else owner
        at = jnp.where(live, step * per_owner + rank, unused)
        image = lax.rem(jnp.maximum(pairs[0, row], 0), img_dev)
        table[at] = image * MARK_BASE + lax.rem(jnp.maximum(partner, 0), img_dev) + 1

    loads[1].wait()
    loads[2].wait()
    embedded = jnp.dot(enc[...], w[...], preferred_element_type=F32).astype(BF16)
    emb[...] = embedded
    stores = [pltpu.make_async_copy(emb, emb_hbm, out_sem.at[0])]
    stores[-1].start()
    normed[...] = layer_norm(embedded.astype(F32)).astype(BF16)
    stores.append(pltpu.make_async_copy(normed, normed_hbm, out_sem.at[1]))
    stores[-1].start()
    row = 0
    for n, steps in enumerate(sets):
        rows = sends[n].shape[0]
        part = filled.at[pl.ds(row, rows)]
        fill(part, normed, table, steps, per_owner, patches)
        stores.append(pltpu.make_async_copy(part, sends[n], out_sem.at[2 + n]))
        stores[-1].start()
        row += rows
    for store in stores:
        store.wait()


def load_kernel(from_ref, to_ref, sem):
    move = pltpu.make_async_copy(from_ref, to_ref, sem)
    move.start()
    move.wait()


def join_kernel(copies, *refs):
    for source, at, target, to, rows in copies:
        refs[2 + target][to : to + rows, :] = refs[source][at : at + rows, :]


def query_kernel(scale, normed_ref, w_ref, out_ref):
    rows = jnp.dot(normed_ref[...], w_ref[...], preferred_element_type=F32).astype(BF16)
    out_ref[...] = rows * jnp.asarray(scale, BF16)


def decode_kernel(
    parts, per_owner, patches, first_call, last_call, query_ref, emb_ref, wk_ref, wv_ref, wo_ref, wh_ref, *rest
):
    rest = list(rest)
    totals_in = None if first_call else rest.pop(0)
    operands = [rest.pop(0) for _ in range(1 + max(n for n, _ in parts))]
    if last_call:
        points_ref, descriptors_ref, confidence_ref, q_rows, e_rows, marks, ids, sem, totals_ref = rest
    else:
        totals_ref, q_rows, e_rows, marks, ids, sem = rest
    width = wk_ref.shape[0]
    pair = 2 * (width // HEADS)
    span = per_owner * patches
    tall = block_rows(per_owner, patches, width)

    rows = []
    for k, (n, block) in enumerate(parts):
        top = block * tall
        mark = operands[n][top + tall - TILE : top + tall, :]
        marks[k * TILE : (k + 1) * TILE, :] = mark.astype(F32).astype(jnp.int32)
        pieces = [operands[n][top + f * span : top + (f + 1) * span, :] for f in range(width // LANES)]
        rows.append(jnp.concatenate(pieces, axis=1))
    to_scalars = pltpu.make_async_copy(marks, ids, sem)
    to_scalars.start()
    x = jnp.concatenate(rows, axis=0) if len(rows) > 1 else rows[0]
    keys = jnp.dot(x, wk_ref[...], preferred_element_type=F32).astype(BF16)
    values = jnp.dot(x, wv_ref[...], preferred_element_type=F32).astype(BF16)

    to_scalars.wait()
    slots = [ids[k * TILE + rank, 0] for k in range(len(parts)) for rank in range(per_owner)]
    for n, mark in enumerate(slots):
        at = pl.ds(pl.multiple_of(jnp.maximum(mark - 1, 0) * patches, patches), patches)
        to = slice(n * patches, (n + 1) * patches)
        q_rows[to, :] = query_ref[at, :]
        e_rows[to, :] = emb_ref[at, :]

    zero = jnp.zeros((), BF16)
    attended = []
    some = span * max(1, LANES // span)
    for start in range(0, x.shape[0], some):
        cut = slice(start, min(start + some, x.shape[0]))
        size = cut.stop - cut.start
        first = lax.broadcasted_iota(jnp.int32, (size, pair), 1) < pair // 2
        at_row = lax.rem(lax.broadcasted_iota(jnp.int32, (2 * size, size), 0), size) // patches
        same = at_row == lax.broadcasted_iota(jnp.int32, (2 * size, size), 1) // patches
        found = []
        for p in range(HEADS // 2):
            cols = slice(p * pair, (p + 1) * pair)
            q = q_rows[cut, cols]
            both = jnp.concatenate([jnp.where(first, q, zero), jnp.where(first, zero, q)], axis=0)
            scores = lax.dot_general(
                both, keys[cut, cols], (((1,), (1,)), ((), ())), preferred_element_type=F32
            )
            exponent = jnp.exp(jnp.where(same, scores, -jnp.inf))
            weights = (exponent / jnp.sum(exponent, axis=-1, keepdims=True)).astype(BF16)
            mixed = jnp.dot(weights, values[cut, cols], preferred_element_type=F32)
            found.append(jnp.where(first, mixed[:size], mixed[size:]).astype(BF16))
        attended.append(jnp.concatenate(found, axis=1))
    attended = jnp.concatenate(attended, axis=0) if len(attended) > 1 else attended[0]
    updated = e_rows[...].astype(F32) + jnp.dot(attended, wo_ref[...], preferred_element_type=F32)
    head_input = layer_norm(updated).astype(BF16)
    head_out = lax.dot_general(
        head_input, wh_ref[...], (((1,), (1,)), ((), ())), preferred_element_type=F32
    )
    weight = 1.0 + jnp.exp(head_out[:, LOGIT : LOGIT + 1])
    column = lax.broadcasted_iota(jnp.int32, head_out.shape, 1)
    terms = jnp.where(column == LOGIT, weight, weight * head_out)
    totals_ref[...] = jnp.zeros(totals_ref.shape, F32) if first_call else totals_in[...]
    for n, mark in enumerate(slots):
        at = pl.ds(pl.multiple_of(jnp.maximum(mark - 1, 0) * patches, patches), patches)
        term = terms[n * patches : (n + 1) * patches, :]
        totals_ref[at, :] = totals_ref[at, :] + jnp.where(mark > 0, term, 0.0)

    if last_call:
        img_dev = confidence_ref.shape[1]
        for token in range(patches):
            rows = jnp.transpose(totals_ref[pl.ds(token, img_dev, stride=patches), :])
            confidence = rows[LOGIT : LOGIT + 1]
            ratio = rows / (1.0 + confidence)
            confidence_ref[token : token + 1, :] = confidence
            points_ref[pl.ds(token, LOGIT, stride=patches), :] = ratio[:LOGIT]
            count = rows.shape[0] - LOGIT - 1
            descriptors_ref[pl.ds(token, count, stride=patches), :] = ratio[LOGIT + 1 :]


def vmem():
    return pl.BlockSpec(memory_space=pltpu.VMEM)


def smem():
    return pl.BlockSpec(memory_space=pltpu.SMEM)


def hbm():
    return pl.BlockSpec(memory_space=pltpu.HBM)


LITTLE = pl.CostEstimate(flops=1, bytes_accessed=1, transcendentals=0)


def per_device(enc_tokens, pair_list, w_embed, w_query, w_key, w_value, w_out, w_head):
    groups = lax.axis_size("img")
    img_dev, patches, enc_width = enc_tokens.shape
    width = w_query.shape[0]
    channels = w_head.shape[1]
    pair_dev = pair_list.shape[0]
    per_owner = (pair_dev + groups - 2) // (groups - 1)
    span = per_owner * patches
    own_rows = img_dev * patches
    params = pltpu.CompilerParams(vmem_limit_bytes=VMEM_LIMIT)
    large = pltpu.CompilerParams(vmem_limit_bytes=LARGE_LIMIT)
    by_permute = groups <= MOST_GROUPS and groups >= 8 and groups & (groups - 1) == 0
    tall = block_rows(per_owner, patches, width)

    def rows_of(count):
        return jax.ShapeDtypeStruct((count, width), BF16)

    def blocks_of(count):
        return jax.ShapeDtypeStruct((count * tall, LANES), BF16)

    chips = groups // 2
    far, near = list(range(chips - 1, chips // 2 - 1, -1)), list(range(1, chips // 2))
    if by_permute:
        sets = [[2 * t + 1 for t in [0] + far], [2 * far[0]], [2 * t for t in far[1:]]]
        sets += [[2 * t + 1 for t in near], [2 * t for t in near]]
    else:
        sets = [list(range(groups))]
    embedded, normed, *sends = pl.pallas_call(
        functools.partial(embed_kernel, groups, per_owner, patches, by_permute, sets),
        out_shape=[rows_of(own_rows)] * 2 + [blocks_of(len(steps)) for steps in sets],
        in_specs=[hbm()] * 3,
        out_specs=[hbm()] * (2 + len(sets)),
        scratch_shapes=[
            pltpu.SMEM((2, pair_dev), jnp.int32),
            pltpu.SMEM((groups * per_owner + 1,), jnp.int32),
            pltpu.SMEM((groups + 1,), jnp.int32),
            pltpu.VMEM((own_rows, enc_width), BF16),
            pltpu.VMEM((enc_width, width), BF16),
            pltpu.VMEM((own_rows, width), BF16),
            pltpu.VMEM((own_rows, width), BF16),
            pltpu.VMEM((sum(len(steps) for steps in sets) * tall, LANES), BF16),
            pltpu.SemaphoreType.DMA((3,)),
            pltpu.SemaphoreType.DMA((2 + len(sets),)),
        ],
        compiler_params=large,
        cost_estimate=LITTLE,
        name="embed",
    )(pair_list.T, enc_tokens.reshape(own_rows, enc_width), w_embed)

    queries = pl.pallas_call(
        functools.partial(query_kernel, 1.0 / math.sqrt(width // HEADS)),
        out_shape=rows_of(own_rows),
        in_specs=[vmem()] * 2,
        out_specs=vmem(),
        compiler_params=params,
        cost_estimate=LITTLE,
        name="queries",
    )(normed, w_query)

    def decode(operands, parts, totals, last_call):
        count = span * len(parts)
        first_call = totals is None
        totals_shape = (own_rows, channels)
        scratch = [pltpu.VMEM((count, width), BF16)] * 2
        scratch.append(pltpu.VMEM((len(parts) * TILE, LANES), jnp.int32))
        scratch.append(pltpu.SMEM((len(parts) * TILE, LANES), jnp.int32))
        scratch.append(pltpu.SemaphoreType.DMA)
        if last_call:
            shapes = [(LOGIT * patches, img_dev), ((channels - 1 - LOGIT) * patches, img_dev), (patches, img_dev)]
            out_shape = [jax.ShapeDtypeStruct(s, F32) for s in shapes]
            out_specs = [vmem()] * 3
            scratch.append(pltpu.VMEM(totals_shape, F32))
        else:
            out_shape, out_specs = jax.ShapeDtypeStruct(totals_shape, F32), vmem()
        inputs = [queries, embedded, w_key, w_value, w_out, w_head.T]
        inputs += ([] if first_call else [totals]) + operands
        return pl.pallas_call(
            functools.partial(decode_kernel, parts, per_owner, patches, first_call, last_call),
            out_shape=out_shape,
            in_specs=[vmem()] * len(inputs),
            out_specs=out_specs,
            scratch_shapes=scratch,
            compiler_params=params,
            cost_estimate=LITTLE,
            name="decode",
        )(*inputs)

    if by_permute:

        def permute(block, step):
            return lax.ppermute(block, "img", [(i, i ^ step) for i in range(groups)])

        mate_far, mate_near = permute(sends[0], 1), permute(sends[3], 1)
        first = permute(sends[1], 2 * far[0])
        own_far = pl.pallas_call(
            load_kernel,
            out_shape=blocks_of(len(far) - 1),
            in_specs=[hbm()],
            out_specs=vmem(),
            scratch_shapes=[pltpu.SemaphoreType.DMA],
            compiler_params=params,
            cost_estimate=LITTLE,
            name="load",
        )(sends[2])

        def join(own, mate, counts, copies):
            copies = [(n, at * tall, target, to * tall, tall) for n, at, target, to in copies]
            return pl.pallas_call(
                functools.partial(join_kernel, copies),
                out_shape=[blocks_of(c) for c in counts],
                in_specs=[vmem()] * 2,
                out_specs=[vmem()] * len(counts),
                compiler_params=params,
                cost_estimate=LITTLE,
                name="join",
            )(own, mate)

        copies = []
        for n in range(len(far) - 1):
            copies += [(0, n, n, 0), (1, n + 2, n, 1)]
        copies.append((1, 1, len(far) - 1, 0))
        *both, late = join(own_far, mate_far, [2] * (len(far) - 1) + [1], copies)
        both = dict(zip(far[1:], both))
        copies = []
        for n in range(len(near)):
            copies += [(0, n, n, 0), (1, n, n, 1)]
        both.update(zip(near, join(sends[4], mate_near, [2] * len(near), copies)))

        got = {far[1]: permute(both[far[1]], 2 * far[1])}
        for n, t in enumerate(near):
            block = both[t]
            if n > 1:
                block, got[near[n - 2]] = lax.optimization_barrier((block, got[near[n - 2]]))
            got[t] = permute(block, 2 * t)
        totals = decode([mate_far], [(0, 0)], None, False)
        block, first, totals = lax.optimization_barrier((both[far[2]], first, totals))
        got[far[2]] = permute(block, 2 * far[2])
        totals = decode([first], [(0, 0)], totals, False)
        for n in range(3, len(far)):
            block, got[far[n - 2]], totals = lax.optimization_barrier((both[far[n]], got[far[n - 2]], totals))
            got[far[n]] = permute(block, 2 * far[n])
        totals = decode([got[far[1]]], [(0, 0), (0, 1)], totals, False)
        late, got[far[-2]], totals = lax.optimization_barrier((late, got[far[-2]], totals))
        last = permute(late, 2 * far[0])
        plan = [near[:2], far[2:3], near[2:]] + [[t] for t in far[3:-1]]
        for pair in plan:
            parts = [(n, m) for n in range(len(pair)) for m in (0, 1)]
            totals = decode([got[t] for t in pair], parts, totals, False)
        totals = decode([got[far[-1]], last], [(0, 0), (0, 1), (1, 0)], totals, True)
    else:
        got = lax.all_to_all(sends[0].reshape(groups, tall, LANES), "img", 0, 0, tiled=True)
        some = math.gcd(groups, max(1, LANES // span))

        def decode_some(k, totals, last_call):
            block = lax.dynamic_slice_in_dim(got, k * some, some).reshape(some * tall, LANES)
            return decode([block], [(0, n) for n in range(some)], totals, last_call)

        totals = lax.fori_loop(
            0,
            groups // some - 1,
            lambda k, totals: decode_some(k, totals, False),
            jnp.zeros((own_rows, channels), F32),
        )
        totals = decode_some(groups // some - 1, totals, True)
    points, descriptors, confidence = totals
    return (
        jnp.transpose(points.reshape(LOGIT, patches, img_dev), (2, 0, 1)),
        jnp.transpose(descriptors.reshape(channels - 1 - LOGIT, patches, img_dev), (2, 0, 1)),
        jnp.transpose(confidence),
    )


def solution(mesh):
    rows = P(("scene", "img"))
    return jax.shard_map(
        per_device,
        mesh=mesh,
        in_specs=(rows, rows, P(), P(), P(), P(), P(), P()),
        out_specs=(rows, rows, rows),
        check_vma=False,
    )
```
